256 devices in a mesh: grp: 8 (over y, z_lo), ep: 32 (over z_hi, x, core).
Axes of the slice: x: 4, y: 4, z: 8 (z_hi: 4, z_lo: 2; z = z_hi * 2 + z_lo), core: 2. Of those that a mesh axis runs over, the one named last changes fastest.
Arguments:
- tokens: bfloat16 [2, 16384, 3584], P(None, ('grp', 'ep')), may hold values from -6 to 6
- expert_ids: int32 [2, 16384, 2], P(None, ('grp', 'ep')), may hold values from 0 to 7, all different within a row; in each aligned block of 64 rows (0 to 63, 64 to 127, ..., all dimensions but the last counted through in order) at most 20 rows name the same one
- gate_weights: float32 [2, 16384, 2], P(None, ('grp', 'ep')), may hold values from 0.1 to 1
- donor_group: int32 [8, 32], replicated, may hold values from 0 to 7
- gate_pieces: bfloat16 [256, 3584, 256], P(('grp', 'ep')), may hold values from -0.09375 to 0.09375
- up_pieces: bfloat16 [256, 3584, 256], P(('grp', 'ep')), may hold values from -0.09375 to 0.09375
- down_pieces: bfloat16 [256, 3584, 256], P(('grp', 'ep')), may hold values from -0.1875 to 0.1875
Outputs:
- mixed: bfloat16 [2, 16384, 3584], P(None, ('grp', 'ep'))
- landed: bfloat16 [3, 114688, 256], P(None, ('grp', 'ep'))
The draws below stay inside these ranges and needn't reach their ends.
Inputs may be any that keep to these rules, and one draw needn't show every extreme that they name: `expert_ids`: within each aligned block of 64 rows (one device's tokens of one micro-batch) no expert is named by more than 20 rows, and that bound is reached; each row names 2 different experts. `donor_group`: A group may name itself, and then the slot takes its own rows.
All inputs are finite; a program needn't handle non-finite values.
Results may differ from the reference program's by a relative error of at most 0.0058.
Values may be sent and summed in bfloat16 or wider, within the bound.
A program may use at most 128 MiB of HBM per device.

```python
import math
from functools import partial
import jax
import jax.numpy as jnp
import numpy as np
from jax import lax

D = 3584
FF = 1024
SPLIT = 4
TOP = 2
MICRO = 2
TOK_DEV = 64
FFP = 256
SPAN = 448
EXPERTS = 8
CAPACITY = 20
TOKENS = 16384
PIECES = 256
N_GRP = 8
N_EP = 32


def with_ends(entries, rng, low, high):
    dims = entries.shape
    spot = [jax.random.randint(jax.random.fold_in(rng, axis), (), 0, dims[axis]) for axis in range(len(dims))]
    entries = entries.at[tuple(spot)].set(low)
    longest = dims.index(max(dims))
    spot[longest] = (spot[longest] + 1) % dims[longest]
    return entries.at[tuple(spot)].set(high)


def level_of(stream_key, dims, cuts, smallest, largest):
    def one(position, parts):
        heights = jax.random.uniform(jax.random.fold_in(jax.random.fold_in(stream_key, 6), position), (parts,), jnp.float32, smallest / len(cuts), largest / len(cuts))
        return jnp.repeat(jnp.exp(heights), dims[position] // parts).reshape((-1,) + (1,) * (len(dims) - position - 1))

    loudness = one(*cuts[0])
    for cut in cuts[1:]:
        loudness = loudness * one(*cut)
    return loudness


def deal_out(rng, own, number, rows, number_of, top, reach, skew):
    ranking = jax.random.permutation(rng, number_of)
    packed, usual = shares(number_of, rows * top, reach, skew, True), shares(number_of, rows * top, reach, skew, False)
    places = jnp.arange(number_of)

    def named(lengths, offset_by):
        used = int((lengths > 0).sum())
        fixed = max(1, used // 4)
        shifted = fixed + (places - fixed + offset_by * (used - fixed)) % max(1, number_of - fixed)
        return jnp.zeros((number_of,), jnp.int32).at[ranking[jnp.where(places < fixed, places, shifted)]].set(jnp.asarray(lengths, jnp.int32))

    lengths = jnp.where(number % 4 == 0, named(packed, number // 4), named(usual, number - number // 4 - 1))
    mixed = jax.random.permutation(jax.random.fold_in(own, 3), number_of)
    giver, receiver = mixed[0:number_of // 2 * 2:2], mixed[1:number_of // 2 * 2:2]
    slack = jnp.minimum(lengths[giver] - 1, reach - lengths[receiver]) // 2
    slack = jnp.where((giver == ranking[0]) | (receiver == ranking[0]) | (lengths[receiver] == 0), 0, jnp.maximum(slack, 0))
    shifted = jax.random.randint(jax.random.fold_in(own, 4), (number_of // 2,), 0, 1 << 20) % (slack + 1)
    lengths = lengths.at[giver].add(-shifted).at[receiver].add(shifted)
    items = jnp.searchsorted(jnp.cumsum(lengths), jnp.arange(rows * top), side="right").astype(jnp.int32)
    grid = items.reshape(top, rows).T
    grid = grid[jax.random.permutation(jax.random.fold_in(own, 1), rows)]
    offset_by = jax.random.randint(jax.random.fold_in(own, 2), (rows, 1), 0, top)
    return jnp.take_along_axis(grid, (jnp.arange(top)[None, :] + offset_by) % top, axis=1)


def shares(amount, total, bound, slope, full):
    portions = [(1 << 20) // math.isqrt(rank ** slope) + 1 for rank in range(1, amount + 1)]
    largest = bound if full else min(bound, max(-(-total // amount), total * portions[0] // sum(portions)))
    least = 1 if total - largest >= amount - 1 else 0
    holding, surplus = [largest] + [least] * (amount - 1), total - largest - least * (amount - 1)
    while surplus > 0:
        free = [i for i in range(1, amount) if holding[i] < largest] or [i for i in range(1, amount) if holding[i] < bound]
        pool, budget = sum([portions[i] for i in free]), surplus
        for i in free:
            addition = min(bound - holding[i], max(1, budget * portions[i] // pool), surplus)
            holding[i] = holding[i] + addition
            surplus = surplus - addition
    return np.array(holding)


def scatter_about(key, dims, width, limit, cuts=(), kind=jnp.bfloat16):
    values = jax.random.normal(key, dims, jnp.float32) * width
    if len(cuts) > 0:
        values = level_of(key, dims, cuts, -0.22, 0.18) * values
    return jnp.clip(values, min=-limit, max=limit).astype(kind)


def setup_inputs(seed: int = 0) -> dict:
    splits = jax.random.split(jax.random.key(seed), 8)
    tokens = scatter_about(splits[0], (MICRO, TOKENS, D), 1.0, 6.0, ((1, 256),))
    expert_ids_keys = jax.random.split(jax.random.fold_in(splits[1], 1), MICRO * TOKENS // TOK_DEV)
    expert_ids_turns = jax.random.permutation(jax.random.fold_in(splits[1], 3), MICRO * TOKENS // TOK_DEV)
    expert_ids = jax.vmap(lambda own, number: deal_out(jax.random.fold_in(splits[1], 2), own, number, TOK_DEV, EXPERTS, TOP, CAPACITY, 2))(expert_ids_keys, expert_ids_turns).reshape((MICRO, TOKENS, TOP))
    gate_weights = jnp.clip(0.1 + 0.9 * jax.random.uniform(splits[2], (MICRO, TOKENS, TOP), jnp.float32) ** level_of(splits[2], (MICRO, TOKENS, TOP), ((1, 256),), -0.2, 0.2), 0.1, 1.0)
    donor_group = with_ends(jax.random.randint(splits[3], (N_GRP, N_EP), 0, N_GRP), jax.random.fold_in(splits[3], 1), 0, N_GRP - 1).astype(jnp.int32)
    gate_pieces = scatter_about(splits[4], (PIECES, D, FFP), D ** -0.5, 0.09375, ((0, 256),))
    up_pieces = scatter_about(splits[5], (PIECES, D, FFP), D ** -0.5, 0.09375, ((0, 256),))
    down_pieces = scatter_about(splits[6], (PIECES, D, FFP), FF ** -0.5, 0.1875, ((0, 256),))
    return {"tokens": tokens, "expert_ids": expert_ids, "gate_weights": gate_weights, "donor_group": donor_group, "gate_pieces": gate_pieces, "up_pieces": up_pieces, "down_pieces": down_pieces}


def slot_table(picked_ids, experts, capacity):
    row_count, chosen = picked_ids.shape
    flat_picks = picked_ids.reshape(row_count * chosen)
    onehot = (flat_picks[:, None] == jnp.arange(experts, dtype=jnp.int32)[None, :]).astype(jnp.int32)
    earlier = jnp.cumsum(onehot, axis=0) - onehot
    slot_ranks = jnp.sum(earlier * onehot, axis=1).astype(jnp.int32)
    slot_index = (flat_picks * capacity + slot_ranks).astype(jnp.int32)
    anchor = (jnp.arange(row_count * chosen, dtype=jnp.int32) // chosen).astype(jnp.int32)
    sources = jnp.zeros((experts * capacity,), jnp.int32).at[slot_index].set(anchor)
    filled = jnp.zeros((experts * capacity,), jnp.int32).at[slot_index].set(1)
    return slot_index.reshape(row_count, chosen), sources, filled


def hidden_units(inputs, gate_part, up_part):
    gate_value = jnp.dot(inputs, gate_part, preferred_element_type=jnp.float32)
    up_value = jnp.dot(inputs, up_part, preferred_element_type=jnp.float32)
    return (jax.nn.silu(gate_value) * up_value).astype(jnp.bfloat16)


def project_down(hidden, down_part):
    return lax.dot_general(hidden, down_part, (((1,), (1,)), ((), ())), preferred_element_type=jnp.float32)


def by_group(array):
    tail_shape = array.shape[2:]
    split_rows = array.reshape((MICRO, N_GRP, N_EP, TOK_DEV) + tail_shape)
    moved = jnp.moveaxis(split_rows, 1, 0)
    return moved.reshape((N_GRP, MICRO * N_EP, TOK_DEV) + tail_shape)


def reference(tokens, expert_ids, gate_weights, donor_group, gate_pieces, up_pieces, down_pieces):
    blocks = MICRO * N_EP
    token_groups = by_group(tokens)
    pick_groups = by_group(expert_ids)
    weight_groups = by_group(gate_weights)
    gate_groups = gate_pieces.reshape(N_GRP, EXPERTS, SPLIT, D, FFP)
    up_groups = up_pieces.reshape(N_GRP, EXPERTS, SPLIT, D, FFP)
    down_groups = down_pieces.reshape(N_GRP, EXPERTS, SPLIT, D, FFP)

    def one_group(operands):
        block_tokens, picks, weights_here, gate_part, up_part, down_part = operands
        slot_index, sources, filled = jax.vmap(partial(slot_table, experts=EXPERTS, capacity=CAPACITY))(picks)
        expert_sources = sources.reshape(blocks, EXPERTS, CAPACITY).transpose(1, 0, 2)
        expert_filled = filled.reshape(blocks, EXPERTS, CAPACITY).transpose(1, 0, 2)

        def one_expert(expert_operands):
            gate_expert, up_expert, down_expert, source_rows, fill_rows = expert_operands
            gathered = jax.vmap(partial(jnp.take, axis=0))(block_tokens, source_rows)
            inputs = jnp.where(fill_rows[:, :, None] > 0, gathered, jnp.zeros_like(gathered)).reshape(blocks * CAPACITY, D)
            total = jnp.zeros((blocks * CAPACITY, D), jnp.float32)
            for split_index in range(SPLIT):
                hidden = hidden_units(inputs, gate_expert[split_index], up_expert[split_index])
                partial_out = lax.optimization_barrier(project_down(hidden, down_expert[split_index]).astype(jnp.bfloat16))
                total = total + partial_out.astype(jnp.float32)
            return total.reshape(blocks, CAPACITY, D)

        sums = lax.map(one_expert, (gate_part, up_part, down_part, expert_sources, expert_filled))

        def one_block(block_operands):
            block_index, slots_here, weights_block = block_operands
            served = lax.dynamic_index_in_dim(sums, block_index, axis=1, keepdims=False)
            flat_out = served.reshape(EXPERTS * CAPACITY, D)
            picked = jnp.take(flat_out, slots_here, axis=0)
            return jnp.sum(weights_block[:, :, None] * picked, axis=1).astype(jnp.bfloat16)

        return lax.map(one_block, (jnp.arange(blocks, dtype=jnp.int32), slot_index, weights_here))

    mixed_groups = lax.map(one_group, (token_groups, pick_groups, weight_groups, gate_groups, up_groups, down_groups))
    mixed = mixed_groups.reshape(N_GRP, MICRO, N_EP, TOK_DEV, D).transpose(1, 0, 2, 3, 4).reshape(MICRO, TOKENS, D)

    slot_columns = jnp.broadcast_to(jnp.arange(N_EP, dtype=jnp.int32)[None, :], (N_GRP, N_EP))

    def copied(pieces):
        rows = pieces[:, :SPAN].reshape(N_GRP, N_EP, SPAN, FFP)
        return rows[donor_group, slot_columns].reshape(PIECES * SPAN, FFP)

    landed = jnp.stack([copied(gate_pieces), copied(up_pieces), copied(down_pieces)], axis=0)
    return mixed, landed
```

```python
import jax
import jax.numpy as jnp
from jax import lax
from jax.experimental import pallas as pl
from jax.experimental.pallas import tpu as pltpu
from jax.sharding import PartitionSpec as P

MESH = pl.DeviceIdType.MESH
D = 3584
F = 256
CAP = 20
HALF = 40
CH = 80
TILE = 512
SPAN = 448
BF = jnp.bfloat16
F32 = jnp.float32


def rows(index, size=CH):
    return pl.ds(pl.multiple_of(index * size, 16), size)


def layer(
    tok_ref, meta_ref, donor_ref, gate_ref, up_ref, down_ref, mixed_ref, landed_ref,
    tok_all, meta_all, onehot, w_hi, w_lo, pack, zin, xin, gw, uw, dw, gacc, uacc, hid,
    part, c1buf, c2buf, zout, zback, acc, ex_send, ex_recv, cand, lsend, lrecv,
    load_sem, s_send, s_recv, z_send, z_recv, x_send, x_recv, r_send,
    c1_send, c1_recv, c2_send, c2_recv, c3_send, zo_recv, b_send, b_recv,
    y_send, y_recv, l_send, l_recv,
):
    grp = lax.axis_index("grp")
    ep = lax.axis_index("ep")
    y, zl = grp // 2, grp % 2
    z, x, c = ep // 8, (ep // 2) % 4, ep % 2
    pair = x // 2
    mate = x + 1 - 2 * (x % 2)
    cross = (x + 2) % 4

    def at(zz, xx, cc):
        return (grp, zz * 8 + xx * 2 + cc)

    sibling = at(z, x, 1 - c)

    def ygroup(d):
        return (((y + d) % 4) * 2 + zl, ep)

    partner = (y * 2 + 1 - zl, ep)

    def remote(src, dst, send, recv, target):
        return pltpu.make_async_remote_copy(
            src_ref=src, dst_ref=dst, send_sem=send, recv_sem=recv,
            device_id=target, device_id_type=MESH,
        )

    pieces = (gate_ref, up_ref, down_ref)
    loads = [
        pltpu.make_async_copy(tok_ref, tok_all.at[pl.ds(0, 128)], load_sem.at[0]),
        pltpu.make_async_copy(gate_ref, gw, load_sem.at[1]),
        pltpu.make_async_copy(up_ref, uw, load_sem.at[2]),
        pltpu.make_async_copy(down_ref, dw, load_sem.at[3]),
    ] + [
        pltpu.make_async_copy(pieces[j].at[pl.ds(0, SPAN)], cand.at[j], load_sem.at[4 + j])
        for j in range(3)
    ]
    for cp in loads:
        cp.start()

    barrier = pltpu.get_barrier_semaphore()
    greeted = [at(z, (x + i) % 4, c) for i in range(1, 4)]
    greeted += [at(z, (x + i) % 4, 1 - c) for i in range(4)]
    greeted += [at((z + i) % 4, x, c) for i in range(1, 4)]
    greeted += [ygroup(i) for i in range(1, 4)]
    greeted += [partner]
    for target in greeted:
        pl.semaphore_signal(barrier, inc=1, device_id=target, device_id_type=MESH)
    pl.semaphore_wait(barrier, len(greeted))

    sib_meta = remote(meta_ref, meta_all, s_send.at[1], s_recv.at[1], sibling)
    sib_meta.start()
    sib_tok = remote(tok_ref, tok_all.at[pl.ds(128, 128)], s_send.at[0], s_recv.at[0], sibling)
    sib_tok.start()
    y_copies = []
    for k, d in enumerate((1, 3, 2)):
        for j in range(3):
            cp = remote(
                pieces[j].at[pl.ds(0, SPAN)], cand.at[((4 - d) % 4) * 3 + j],
                y_send.at[k * 3 + j], y_recv.at[(d - 1) * 3 + j], ygroup(d),
            )
            cp.start()
            y_copies.append(cp)

    sib_meta.wait_recv()
    row8 = lax.broadcasted_iota(jnp.int32, (8, 128), 0)
    lane8 = lax.broadcasted_iota(jnp.int32, (8, 128), 1)
    expert = (2 * ((row8 + z) % 4) + c).astype(F32)
    first = lax.broadcasted_iota(jnp.int32, (128, 128), 0)
    second = lax.broadcasted_iota(jnp.int32, (128, 128), 1)
    before = jnp.where((first < second) & (first // 64 == second // 64), 1.0, 0.0).astype(BF)
    slot = lax.broadcasted_iota(jnp.int32, (CH, 128), 0).astype(F32)
    for h, meta in enumerate((meta_ref, meta_all)):
        id0, id1 = meta[0:1, :], meta[1:2, :]
        w0, w1 = meta[2:3, :], meta[3:4, :]
        hit0, hit1 = expert == id0, expert == id1
        named = jnp.where(hit0 | hit1, 1.0, 0.0)
        rank = jnp.dot(named.astype(BF), before, preferred_element_type=F32)
        place = rank + jnp.where(lane8 >= 64, float(CAP), 0.0) + float(HALF * h)
        place = jnp.where(named > 0.0, place, -1.0)
        weight = jnp.where(hit0, w0, jnp.where(hit1, w1, 0.0))
        for d in range(4):
            match = place[d : d + 1, :] == slot
            ww = jnp.where(match, weight[d : d + 1, :], 0.0)
            hi = ww.astype(BF)
            onehot[pl.ds(d * CH, CH), pl.ds(h * 128, 128)] = jnp.where(match, 1.0, 0.0).astype(BF)
            w_hi[pl.ds(d * CH, CH), pl.ds(h * 128, 128)] = hi
            w_lo[pl.ds(d * CH, CH), pl.ds(h * 128, 128)] = (ww - hi.astype(F32)).astype(BF)

    loads[0].wait()
    sib_tok.wait_recv()

    def tiles(body):
        def step(i, carry):
            body(pl.ds(pl.multiple_of(i * TILE, TILE), TILE))
            return carry

        lax.fori_loop(0, D // TILE, step, 0)

    def pack_chunk(d):
        def body(cols):
            pack[pl.ds(d * CH, CH), cols] = jnp.dot(
                onehot[pl.ds(d * CH, CH), :], tok_all[:, cols], preferred_element_type=F32
            ).astype(BF)

        tiles(body)

    def z_copy(d):
        return remote(
            pack.at[pl.ds(d * CH, CH)], zin.at[pl.ds((d - 1) * CH, CH)],
            z_send.at[d - 1], z_recv.at[d - 1], at((z + d) % 4, x, c),
        )

    z_copies = {d: z_copy(d) for d in (1, 2, 3)}
    for d in (1, 3):
        pack_chunk(d)
        z_copies[d].start()
    pack_chunk(0)

    serve = 1 - (pair + c) % 2

    def fan(q):
        src = pack.at[pl.ds(0, CH)] if q == 0 else zin.at[pl.ds((q - 1) * CH, CH)]
        dst = xin.at[rows(q * 4 + x)]
        f = (q + x) % 2
        t0 = at(z, serve * mate + (1 - serve) * (2 * c), f)
        t1 = at(
            z, serve * x + (1 - serve) * (2 * c + 1), serve * (1 - c) + (1 - serve) * f
        )
        return (
            remote(src, dst, x_send.at[q * 2], x_recv.at[q * 4 + x], t0),
            remote(src, dst, x_send.at[q * 2 + 1], x_recv.at[q * 4 + x], t1),
            pltpu.make_async_copy(src, dst, x_recv.at[q * 4 + x]),
        )

    def fan_start(q):
        first_copy, second_copy, local = fan(q)
        first_copy.start()
        second_copy.start()

        @pl.when(serve == 1)
        def _():
            local.start()

    def even(q):
        return 1 - (x + c + q) % 2

    def x_wait(q, xs):
        ref = xin.at[rows(q * 4 + xs)]
        pltpu.make_async_copy(ref, ref, x_recv.at[q * 4 + xs]).wait()

    def relay(q, xs):
        ref = xin.at[rows(q * 4 + xs)]
        return remote(ref, ref, r_send.at[q * 4 + xs], x_recv.at[q * 4 + xs], sibling)

    def fan_recv(q):
        x1, x2, x3 = (x + 1) % 4, (x + 2) % 4, (x + 3) % 4

        @pl.when(even(q) == 1)
        def _():
            x_wait(q, x2)
            relay(q, x2).start()
            x_wait(q, x1)
            x_wait(q, x3)

        @pl.when(even(q) == 0)
        def _():
            x_wait(q, x1)
            relay(q, x1).start()
            x_wait(q, x3)
            relay(q, x3).start()
            x_wait(q, x2)

        x_wait(q, x)

    def compute(q):
        r = pl.ds(q * 4 * CH, 4 * CH)
        gacc[...] = jnp.zeros_like(gacc)
        uacc[...] = jnp.zeros_like(uacc)

        def up_body(cols):
            a = xin[r, cols]
            gacc[...] += jnp.dot(a, gw[cols, :], preferred_element_type=F32)
            uacc[...] += jnp.dot(a, uw[cols, :], preferred_element_type=F32)

        tiles(up_body)
        g = gacc[...]
        hid[...] = (g / (1.0 + jnp.exp(-g)) * uacc[...]).astype(BF)

        def down_body(cols):
            part[r, cols] = lax.dot_general(
                hid[...], dw[cols, :], (((1,), (1,)), ((), ())), preferred_element_type=F32
            ).astype(BF)

        tiles(down_body)

    def keep_of(q, own):
        u = even(q) if own else 1 - even(q)
        return u * x + (1 - u) * (3 - x)

    def send_of(q, own):
        u = even(q) if own else 1 - even(q)
        return u * cross + (1 - u) * mate

    def c1(q):
        return (
            remote(
                part.at[rows(q * 4 + send_of(q, False))], c1buf.at[pl.ds((q * 2 + 1) * CH, CH)],
                c1_send.at[q * 2 + 1], c1_recv.at[q * 2 + 1], sibling,
            ),
            remote(
                part.at[rows(q * 4 + keep_of(q, False))], c1buf.at[pl.ds(q * 2 * CH, CH)],
                c1_send.at[q * 2], c1_recv.at[q * 2], sibling,
            ),
        )

    def c1_start(q):
        for cp in c1(q):
            cp.start()

    def c2(q):
        return remote(
            part.at[rows(q * 4 + send_of(q, True))], c2buf.at[pl.ds(q * CH, CH)],
            c2_send.at[q], c2_recv.at[q], at(z, mate, c),
        )

    def add_rows(base, buffers):
        def step(i, carry):
            here = pl.ds(pl.multiple_of(base + i * 16, 16), 16)
            total = part[here, :].astype(F32)
            for buf, offset in buffers:
                total += buf[pl.ds(pl.multiple_of(offset + i * 16, 16), 16), :].astype(F32)
            part[here, :] = total.astype(BF)
            return carry

        lax.fori_loop(0, CH // 16, step, 0)

    def c2_start(q):
        c1(q)[0].wait_recv()
        add_rows((q * 4 + send_of(q, True)) * CH, [(c1buf, (q * 2 + 1) * CH)])
        c2(q).start()

    def c3(q):
        src, dst = part.at[rows(q * 4 + keep_of(q, True))], zout.at[pl.ds(q * CH, CH)]
        u = even(q)
        return (
            remote(
                src, dst, c3_send.at[q], zo_recv.at[q], at(z, u * x + (1 - u) * (3 - x), pair)
            ),
            pltpu.make_async_copy(src, dst, zo_recv.at[q]),
            u * serve,
        )

    def c3_start(q):
        c1(q)[1].wait_recv()
        c2(q).wait_recv()
        add_rows(
            (q * 4 + keep_of(q, True)) * CH, [(c1buf, q * 2 * CH), (c2buf, q * CH)]
        )
        away, local, here = c3(q)

        @pl.when(here == 1)
        def _():
            local.start()

        @pl.when(here == 0)
        def _():
            away.start()

    def zout_wait(q):
        ref = zout.at[pl.ds(q * CH, CH)]
        pltpu.make_async_copy(ref, ref, zo_recv.at[q]).wait()

    def back(q):
        return remote(
            zout.at[pl.ds(q * CH, CH)], zback.at[pl.ds((q - 1) * CH, CH)],
            b_send.at[q - 1], b_recv.at[q - 1], at((z + 4 - q) % 4, x, c),
        )

    def mix(q, start):
        src, base = (zout, 0) if q == 0 else (zback, (q - 1) * CH)
        dims = (((0,), (0,)), ((), ()))

        def body(cols):
            b = src[pl.ds(base, CH), cols]
            r = pl.ds(q * CH, CH)
            value = lax.dot_general(w_hi[r, :], b, dims, preferred_element_type=F32)
            value += lax.dot_general(w_lo[r, :], b, dims, preferred_element_type=F32)
            acc[:, cols] = value if start else acc[:, cols] + value

        tiles(body)

    fan_start(0)
    pack_chunk(2)
    for k in (1, 2, 3):
        loads[k].wait()
    fan_recv(0)
    compute(0)
    c1_start(0)
    c2_start(0)
    for d in (1, 3):
        z_copies[d].wait_send()
    z_copies[2].start()
    for q in (1, 3):
        z_copies[q].wait_recv()
        fan_start(q)
    c3_start(0)

    for j in range(3):
        loads[4 + j].wait()
    for cp in y_copies:
        cp.wait_send()
    for d in (1, 2, 3):
        for j in range(3):
            ref = cand.at[((4 - d) % 4) * 3 + j]
            pltpu.make_async_copy(ref, ref, y_recv.at[(d - 1) * 3 + j]).wait()
    asked = donor_ref[y * 2 + 1 - zl, ep]
    asked_y = (asked // 2 + 4 - y) % 4
    for j in range(3):
        lsend[j] = cand[asked_y * 3 + j]
    l_copy = remote(lsend, lrecv, l_send, l_recv, partner)

    for q in (1, 3):
        fan_recv(q)
        compute(q)
        c1_start(q)
    for q in (1, 3):
        c2_start(q)
    z_copies[2].wait_recv()
    fan_start(2)
    l_copy.start()
    for q in (1, 3):
        c3_start(q)
    zout_wait(0)
    mix(0, True)
    for q in (1, 3):
        zout_wait(q)
        back(q).start()
    fan_recv(2)
    compute(2)
    c1_start(2)
    c2_start(2)
    c3_start(2)
    zout_wait(2)
    back(2).start()
    l_copy.wait()
    wanted = donor_ref[grp, ep]
    wanted_y = (wanted // 2 + 4 - y) % 4
    wanted_z = wanted % 2
    for j in range(3):
        near = cand[wanted_y * 3 + j].astype(F32)
        far = lrecv[j].astype(F32)
        from_here = jnp.full((SPAN, F), wanted_z, jnp.int32) == zl
        landed_ref[j] = jnp.where(from_here, near, far).astype(BF)
    for q in (1, 3, 2):
        back(q).wait_recv()
        mix(q, False)

    def cut(cols):
        ex_send[:, cols] = acc[pl.ds(128, 128), cols].astype(BF)

    tiles(cut)
    swap = remote(ex_send, ex_recv, s_send.at[2], s_recv.at[2], sibling)
    swap.start()
    swap.wait()

    def join(cols):
        mixed_ref[:, cols] = (
            acc[pl.ds(0, 128), cols] + ex_recv[:, cols].astype(F32)
        ).astype(BF)

    tiles(join)

    sib_meta.wait_send()
    sib_tok.wait_send()
    z_copies[2].wait_send()
    for q in range(4):
        first_copy, second_copy, _ = fan(q)
        first_copy.wait_send()
        second_copy.wait_send()

        @pl.when(even(q) == 1)
        def _():
            relay(q, (x + 2) % 4).wait_send()

        @pl.when(even(q) == 0)
        def _():
            relay(q, (x + 1) % 4).wait_send()
            relay(q, (x + 3) % 4).wait_send()

        for cp in c1(q):
            cp.wait_send()
        c2(q).wait_send()
        away, _, here = c3(q)

        @pl.when(here == 0)
        def _():
            away.wait_send()

        if q:
            back(q).wait_send()


def on_device(tokens, expert_ids, gate_weights, donor_group, gate_pieces, up_pieces, down_pieces):
    tok = tokens.reshape(128, D)
    ids = expert_ids.reshape(128, 2).T.astype(F32)
    wts = gate_weights.reshape(128, 2).T
    meta = jnp.concatenate([ids, wts, jnp.zeros((4, 128), F32)], axis=0)
    vmem, hbm = pltpu.VMEM, pl.ANY
    dma = pltpu.SemaphoreType.DMA
    mixed, landed = pl.pallas_call(
        layer,
        out_shape=(
            jax.ShapeDtypeStruct((128, D), BF),
            jax.ShapeDtypeStruct((3, SPAN, F), BF),
        ),
        in_specs=[
            pl.BlockSpec(memory_space=hbm),
            pl.BlockSpec(memory_space=vmem),
            pl.BlockSpec(memory_space=pltpu.SMEM),
            pl.BlockSpec(memory_space=hbm),
            pl.BlockSpec(memory_space=hbm),
            pl.BlockSpec(memory_space=hbm),
        ],
        out_specs=(pl.BlockSpec(memory_space=vmem), pl.BlockSpec(memory_space=vmem)),
        scratch_shapes=[
            vmem((256, D), BF),
            vmem((8, 128), F32),
            vmem((4 * CH, 256), BF),
            vmem((4 * CH, 256), BF),
            vmem((4 * CH, 256), BF),
            vmem((4 * CH, D), BF),
            vmem((3 * CH, D), BF),
            vmem((16 * CH, D), BF),
            vmem((D, F), BF),
            vmem((D, F), BF),
            vmem((D, F), BF),
            vmem((4 * CH, F), F32),
            vmem((4 * CH, F), F32),
            vmem((4 * CH, F), BF),
            vmem((16 * CH, D), BF),
            vmem((8 * CH, D), BF),
            vmem((4 * CH, D), BF),
            vmem((4 * CH, D), BF),
            vmem((3 * CH, D), BF),
            vmem((256, D), F32),
            vmem((128, D), BF),
            vmem((128, D), BF),
            vmem((12, SPAN, F), BF),
            vmem((3, SPAN, F), BF),
            vmem((3, SPAN, F), BF),
            dma((7,)),
            dma((3,)), dma((3,)),
            dma((3,)), dma((3,)),
            dma((8,)), dma((16,)), dma((16,)),
            dma((8,)), dma((8,)),
            dma((4,)), dma((4,)),
            dma((4,)), dma((4,)),
            dma((3,)), dma((3,)),
            dma((9,)), dma((9,)),
            dma, dma,
        ],
        compiler_params=pltpu.CompilerParams(
            collective_id=0, has_side_effects=True, vmem_limit_bytes=62 * 2**20
        ),
        cost_estimate=pl.CostEstimate(
            flops=8 * 10**9, bytes_accessed=10**7, transcendentals=4 * 10**5
        ),
    )(tok, meta, donor_group, gate_pieces[0], up_pieces[0], down_pieces[0])
    return mixed.reshape(2, 64, D), landed


def solution(mesh):
    in_specs = (
        P(None, ("grp", "ep"), None),
        P(None, ("grp", "ep"), None),
        P(None, ("grp", "ep"), None),
        P(),
        P(("grp", "ep"), None, None),
        P(("grp", "ep"), None, None),
        P(("grp", "ep"), None, None),
    )
    out_specs = (P(None, ("grp", "ep"), None), P(None, ("grp", "ep"), None))
    return jax.shard_map(
        on_device, mesh=mesh, in_specs=in_specs, out_specs=out_specs, check_vma=False
    )
```

```python
import jax
import jax.numpy as jnp
from jax import lax
from jax.experimental import pallas as pl
from jax.experimental.pallas import tpu as pltpu
from jax.sharding import PartitionSpec as P

MESH = pl.DeviceIdType.MESH
D = 3584
F = 256
CAP = 20
HALF = 40
CH = 80
K = 2
WIDE = D // K
TILE = 896
LEN = (48, 32)
OFF = (0, 48)
SPAN = 448
BF = jnp.bfloat16
F32 = jnp.float32


def rows(index, size=CH):
    return pl.ds(pl.multiple_of(index * size, 16), size)


def layer(
    tok_ref, meta_ref, donor_ref, gate_ref, up_ref, down_ref, mixed_ref, landed_ref,
    tok_all, meta_all, onehot, weight_t, pack, zin, xin, gw, uw, dw, gacc, uacc, hid,
    part, c1buf, c2buf, zout, home, acc, ex_send, ex_recv, cand, lsend, lrecv,
    load_sem, m_send, m_recv, t_send, t_recv, z_send, z_recv, x_send, x_recv, r_send,
    c1_send, c1_recv, c2_send, c2_recv, c3_send, zo_recv, b_send, b_recv,
    y_send, y_recv, l_send, l_recv, e_send, e_recv,
):
    grp = lax.axis_index("grp")
    ep = lax.axis_index("ep")
    y, zl = grp // 2, grp % 2
    z, x, c = ep // 8, (ep // 2) % 4, ep % 2
    pair = x // 2
    mate = x + 1 - 2 * (x % 2)
    cross = (x + 2) % 4
    near = 3 - x
    serve = 1 - (pair + c) % 2

    def at(zz, xx, cc):
        return (grp, zz * 8 + xx * 2 + cc)

    sibling = at(z, x, 1 - c)

    def ygroup(d):
        return (((y + d) % 4) * 2 + zl, ep)

    partner = (y * 2 + 1 - zl, ep)

    def remote(src, dst, send, recv, target):
        return pltpu.make_async_remote_copy(
            src_ref=src, dst_ref=dst, send_sem=send, recv_sem=recv,
            device_id=target, device_id_type=MESH,
        )

    def arrived(ref, sem):
        pltpu.make_async_copy(ref, ref, sem).wait()

    def piece(k):
        return pl.ds(k * WIDE, WIDE)

    def chunk(q, r, sides=1):
        return pl.ds(sides * (q * CH + OFF[r]), sides * LEN[r])

    def side(q, r, sides, i):
        base = sides * (q * CH + OFF[r])
        return pl.ds(pl.multiple_of(base + i * LEN[r], 16), LEN[r])

    pieces = (gate_ref, up_ref, down_ref)
    loads = [
        pltpu.make_async_copy(tok_ref, tok_all.at[pl.ds(0, 128)], load_sem.at[0]),
        pltpu.make_async_copy(gate_ref, gw, load_sem.at[1]),
        pltpu.make_async_copy(up_ref, uw, load_sem.at[2]),
        pltpu.make_async_copy(down_ref, dw, load_sem.at[3]),
    ] + [
        pltpu.make_async_copy(pieces[j].at[pl.ds(0, SPAN)], cand.at[j], load_sem.at[4 + j])
        for j in range(3)
    ]
    for cp in loads:
        cp.start()

    barrier = pltpu.get_barrier_semaphore()
    greeted = [at(z, x, 1 - c)]
    greeted += [at(z, (x + i) % 4, c) for i in range(1, 4)]
    greeted += [at(z, (x + i) % 4, 1 - c) for i in range(1, 4)]
    greeted += [at((z + i) % 4, x, c) for i in range(1, 4)]
    greeted += [ygroup(i) for i in range(1, 4)]
    greeted += [partner]
    for target in greeted:
        pl.semaphore_signal(barrier, inc=1, device_id=target, device_id_type=MESH)
    pl.semaphore_wait(barrier, len(greeted))

    sib_meta = remote(meta_ref, meta_all, m_send, m_recv, sibling)
    sib_meta.start()

    def sib_tok(k):
        return remote(
            tok_ref.at[:, piece(k)], tok_all.at[pl.ds(128, 128), piece(k)],
            t_send.at[k], t_recv.at[k], sibling,
        )

    for k in range(K):
        sib_tok(k).start()
    y_copies = []
    for n, d in enumerate((1, 3, 2)):
        for j in range(3):
            cp = remote(
                pieces[j].at[pl.ds(0, SPAN)], cand.at[((4 - d) % 4) * 3 + j],
                y_send.at[n * 3 + j], y_recv.at[(d - 1) * 3 + j], ygroup(d),
            )
            cp.start()
            y_copies.append(cp)

    sib_meta.wait_recv()
    row8 = lax.broadcasted_iota(jnp.int32, (8, 128), 0)
    lane8 = lax.broadcasted_iota(jnp.int32, (8, 128), 1)
    expert = (2 * ((row8 + z) % 4) + c).astype(F32)
    first = lax.broadcasted_iota(jnp.int32, (128, 128), 0)
    second = lax.broadcasted_iota(jnp.int32, (128, 128), 1)
    before = jnp.where((first < second) & (first // 64 == second // 64), 1.0, 0.0).astype(BF)
    slot = lax.broadcasted_iota(jnp.int32, (CH, 128), 0).astype(F32)
    for h, meta in enumerate((meta_ref, meta_all)):
        id0, id1 = meta[0:1, :], meta[1:2, :]
        w0, w1 = meta[2:3, :], meta[3:4, :]
        hit0, hit1 = expert == id0, expert == id1
        named = jnp.where(hit0 | hit1, 1.0, 0.0)
        rank = jnp.dot(named.astype(BF), before, preferred_element_type=F32)
        place = rank + jnp.where(lane8 >= 64, float(CAP), 0.0) + float(HALF * h)
        place = jnp.where(named > 0.0, place, -1.0)
        weight = jnp.where(hit0, w0, jnp.where(hit1, w1, 0.0))
        for d in range(4):
            match = place[d : d + 1, :] == slot
            here = (pl.ds(d * CH, CH), pl.ds(h * 128, 128))
            onehot[here] = jnp.where(match, 1.0, 0.0).astype(BF)
            weight_t[here] = jnp.where(match, weight[d : d + 1, :], 0.0).astype(BF)

    loads[0].wait()

    def tiles(body, start=0, size=D):
        def step(i, carry):
            body(pl.ds(pl.multiple_of(start + i * TILE, 128), TILE))
            return carry

        lax.fori_loop(0, size // TILE, step, 0)

    def pack_chunk(d, k):
        def body(cols):
            pack[pl.ds(d * CH, CH), cols] = jnp.dot(
                onehot[pl.ds(d * CH, CH), :], tok_all[:, cols], preferred_element_type=F32
            ).astype(BF)

        tiles(body, k * WIDE, WIDE)

    def z_copy(d, r):
        n = (d - 1) * 2 + r
        return remote(
            pack.at[chunk(d, r)], zin.at[chunk(d - 1, r)],
            z_send.at[n], z_recv.at[n], at((z + d) % 4, x, c),
        )

    def fan(q, r):
        src = pack.at[chunk(0, r)]
        if q:
            src = zin.at[chunk(q - 1, r)]
        dst = xin.at[side(q, r, 4, x)]
        f = (q // 2 + x + r) % 2
        n = q * 2 + r
        recv = x_recv.at[n * 4 + x]
        t0 = at(z, serve * mate + (1 - serve) * near, f)
        return (
            remote(src, dst, x_send.at[n * 2], recv, t0),
            remote(src, dst, x_send.at[n * 2 + 1], recv, sibling),
            pltpu.make_async_copy(src, dst, recv),
            remote(src, dst, x_send.at[n * 2 + 1], recv, at(z, cross, f)),
        )

    def fan_start(q, r):
        away, over, local, beyond = fan(q, r)
        away.start()

        @pl.when(serve == 1)
        def _():
            over.start()
            local.start()

        @pl.when(serve == 0)
        def _():
            beyond.start()

    def even(q, r):
        return 1 - (x + c + q // 2 + r) % 2

    def x_wait(q, r, xs):
        arrived(xin.at[side(q, r, 4, xs)], x_recv.at[(q * 2 + r) * 4 + xs])

    def relay(q, r, xs):
        ref = xin.at[side(q, r, 4, xs)]
        n = (q * 2 + r) * 4 + xs
        return remote(ref, ref, r_send.at[n], x_recv.at[n], sibling)

    def relay_near(q, r):
        @pl.when(even(q, r) == 0)
        def _():
            x_wait(q, r, near)
            relay(q, r, near).start()

    def relay_rest(q, r):
        @pl.when(even(q, r) == 0)
        def _():
            x_wait(q, r, mate)
            relay(q, r, mate).start()

        @pl.when(even(q, r) == 1)
        def _():
            x_wait(q, r, cross)
            relay(q, r, cross).start()

    def up(q, r):
        @pl.when(even(q, r) == 0)
        def _():
            x_wait(q, r, cross)

        @pl.when(even(q, r) == 1)
        def _():
            x_wait(q, r, near)
            x_wait(q, r, mate)

        x_wait(q, r, x)
        o = chunk(q, r, 4)
        s = pl.ds(0, 4 * LEN[r])
        gacc[s, :] = jnp.zeros((4 * LEN[r], F), F32)
        uacc[s, :] = jnp.zeros((4 * LEN[r], F), F32)

        def body(cols):
            a = xin[o, cols]
            gacc[s, :] += jnp.dot(a, gw[cols, :], preferred_element_type=F32)
            uacc[s, :] += jnp.dot(a, uw[cols, :], preferred_element_type=F32)

        tiles(body)
        g = gacc[s, :]
        hid[o, :] = (g / (1.0 + jnp.exp(-g)) * uacc[s, :]).astype(BF)

    def keep_of(q, r, own):
        u = even(q, r) if own else 1 - even(q, r)
        return u * x + (1 - u) * near

    def send_of(q, r, own):
        u = even(q, r) if own else 1 - even(q, r)
        return u * cross + (1 - u) * mate

    def c1(q, r):
        n = (q * 2 + r) * 2
        return (
            remote(
                part.at[side(q, r, 4, send_of(q, r, False))],
                c1buf.at[side(q, r, 2, 1)],
                c1_send.at[n + 1], c1_recv.at[n + 1], sibling,
            ),
            remote(
                part.at[side(q, r, 4, keep_of(q, r, False))],
                c1buf.at[side(q, r, 2, 0)],
                c1_send.at[n], c1_recv.at[n], sibling,
            ),
        )

    def down(q, r):
        o = chunk(q, r, 4)

        def body(cols):
            part[o, cols] = lax.dot_general(
                hid[o, :], dw[cols, :], (((1,), (1,)), ((), ())), preferred_element_type=F32
            ).astype(BF)

        tiles(body)
        for cp in c1(q, r):
            cp.start()

    def c2(q, r):
        n = q * 2 + r
        return remote(
            part.at[side(q, r, 4, send_of(q, r, True))],
            c2buf.at[chunk(q, r)],
            c2_send.at[n], c2_recv.at[n], at(z, mate, c),
        )

    def add_rows(target, buffers, count):
        def step(i, carry):
            total = part[pl.ds(pl.multiple_of(target.start + i * 16, 16), 16), :].astype(F32)
            for buf, other in buffers:
                total += buf[pl.ds(pl.multiple_of(other.start + i * 16, 16), 16), :].astype(F32)
            part[pl.ds(pl.multiple_of(target.start + i * 16, 16), 16), :] = total.astype(BF)
            return carry

        lax.fori_loop(0, count // 16, step, 0)

    def c2_start(q, r):
        c1(q, r)[0].wait_recv()
        add_rows(side(q, r, 4, send_of(q, r, True)), [(c1buf, side(q, r, 2, 1))], LEN[r])
        c2(q, r).start()

    def c3(q, r):
        src = part.at[side(q, r, 4, keep_of(q, r, True))]
        dst = home.at[chunk(0, r)]
        if q:
            dst = zout.at[chunk(q - 1, r)]
        u = even(q, r)
        n = q * 2 + r
        return (
            remote(src, dst, c3_send.at[n], zo_recv.at[n], at(z, u * x + (1 - u) * near, pair)),
            pltpu.make_async_copy(src, dst, zo_recv.at[n]),
            u * serve,
        )

    def c3_start(q, r):
        c1(q, r)[1].wait_recv()
        c2(q, r).wait_recv()
        add_rows(
            side(q, r, 4, keep_of(q, r, True)),
            [(c1buf, side(q, r, 2, 0)), (c2buf, chunk(q, r))],
            LEN[r],
        )
        away, local, here = c3(q, r)

        @pl.when(here == 1)
        def _():
            local.start()

        @pl.when(here == 0)
        def _():
            away.start()

    def back(q, r):
        n = (q - 1) * 2 + r
        return remote(
            zout.at[chunk(q - 1, r)], home.at[chunk(q, r)],
            b_send.at[n], b_recv.at[n], at((z + 4 - q) % 4, x, c),
        )

    def back_start(q, r):
        arrived(zout.at[chunk(q - 1, r)], zo_recv.at[q * 2 + r])
        back(q, r).start()

    def swap(k):
        return remote(
            ex_send.at[:, piece(k)], ex_recv.at[:, piece(k)], e_send.at[k], e_recv.at[k], sibling
        )

    def mix(q, parts, start=False, last=False):
        for r in parts:
            if q:
                back(q, r).wait_recv()
            else:
                arrived(home.at[chunk(0, r)], zo_recv.at[r])
        s = chunk(q, 0) if len(parts) == 1 else pl.ds(q * CH, CH)
        if parts == (1,):
            s = chunk(q, 1)

        def body(cols):
            value = lax.dot_general(
                weight_t[s, :], home[s, cols], (((0,), (0,)), ((), ())),
                preferred_element_type=F32,
            )
            if not start:
                value += acc[:, cols]
            if last:
                acc[pl.ds(0, 128), cols] = value[:128]
                ex_send[:, cols] = value[128:].astype(BF)
            else:
                acc[:, cols] = value

        for k in range(K):
            tiles(body, k * WIDE, WIDE)
            if last:
                swap(k).start()

    def join(k):
        swap(k).wait()

        def body(cols):
            mixed_ref[:, cols] = (
                acc[pl.ds(0, 128), cols] + ex_recv[:, cols].astype(F32)
            ).astype(BF)

        tiles(body, k * WIDE, WIDE)

    def pick():
        for j in range(3):
            loads[4 + j].wait()
        for cp in y_copies:
            cp.wait_send()
        for d in (1, 2, 3):
            for j in range(3):
                arrived(cand.at[((4 - d) % 4) * 3 + j], y_recv.at[(d - 1) * 3 + j])
        asked = donor_ref[y * 2 + 1 - zl, ep]
        asked_y = (asked // 2 + 4 - y) % 4
        for j in range(3):
            lsend[j] = cand[asked_y * 3 + j]

    l_copy = remote(lsend, lrecv, l_send, l_recv, partner)

    def land():
        l_copy.wait()
        wanted = donor_ref[grp, ep]
        wanted_y = (wanted // 2 + 4 - y) % 4
        wanted_z = wanted % 2
        from_here = jnp.full((SPAN, F), wanted_z, jnp.int32) == zl
        for j in range(3):
            close = cand[wanted_y * 3 + j].astype(F32)
            far = lrecv[j].astype(F32)
            landed_ref[j] = jnp.where(from_here, close, far).astype(BF)

    sib_tok(0).wait_recv()
    pack_chunk(2, 0)
    pack_chunk(0, 0)
    sib_tok(1).wait_recv()
    pack_chunk(2, 1)
    z_copy(2, 0).start()
    z_copy(2, 1).start()
    pack_chunk(0, 1)
    fan_start(0, 0)
    fan_start(0, 1)
    pack_chunk(1, 0)
    pack_chunk(1, 1)
    z_copy(1, 0).start()
    pack_chunk(3, 0)
    pack_chunk(3, 1)
    z_copy(3, 0).start()
    z_copy(1, 1).start()
    z_copy(3, 1).start()
    relay_near(0, 0)
    for n in (1, 2, 3):
        loads[n].wait()
    relay_rest(0, 0)
    relay_near(0, 1)
    up(0, 0)
    down(0, 0)
    relay_rest(0, 1)
    c2_start(0, 0)
    up(0, 1)
    down(0, 1)
    z_copy(2, 0).wait_recv()
    fan_start(2, 0)
    c2_start(0, 1)
    relay_near(2, 0)
    relay_rest(2, 0)
    c3_start(0, 0)
    z_copy(2, 1).wait_recv()
    fan_start(2, 1)
    up(2, 0)
    down(2, 0)
    c3_start(0, 1)
    c2_start(2, 0)
    relay_near(2, 1)
    relay_rest(2, 1)
    pick()
    up(2, 1)
    down(2, 1)
    mix(0, (0, 1), start=True)
    c2_start(2, 1)
    z_copy(1, 0).wait_recv()
    fan_start(1, 0)
    z_copy(3, 0).wait_recv()
    fan_start(3, 0)
    c3_start(2, 0)
    back_start(2, 0)
    relay_near(1, 0)
    relay_near(3, 0)
    relay_rest(1, 0)
    relay_rest(3, 0)
    c3_start(2, 1)
    back_start(2, 1)
    z_copy(1, 1).wait_recv()
    fan_start(1, 1)
    z_copy(3, 1).wait_recv()
    fan_start(3, 1)
    l_copy.start()
    up(1, 0)
    down(1, 0)
    up(3, 0)
    down(3, 0)
    relay_near(1, 1)
    relay_near(3, 1)
    c2_start(1, 0)
    c2_start(3, 0)
    relay_rest(1, 1)
    relay_rest(3, 1)
    up(1, 1)
    down(1, 1)
    up(3, 1)
    down(3, 1)
    c2_start(1, 1)
    c2_start(3, 1)
    c3_start(1, 0)
    back_start(1, 0)
    c3_start(3, 0)
    back_start(3, 0)
    land()
    mix(2, (0, 1))
    c3_start(1, 1)
    back_start(1, 1)
    c3_start(3, 1)
    back_start(3, 1)
    mix(1, (0,))
    mix(3, (0,))
    mix(1, (1,))
    mix(3, (1,), last=True)
    join(0)
    join(1)
    sib_meta.wait_send()
    for k in range(K):
        sib_tok(k).wait_send()
    for q in range(4):
        for r in range(2):
            away, over, _, beyond = fan(q, r)
            away.wait_send()

            @pl.when(serve == 1)
            def _():
                over.wait_send()

            @pl.when(serve == 0)
            def _():
                beyond.wait_send()

            @pl.when(even(q, r) == 1)
            def _():
                relay(q, r, cross).wait_send()

            @pl.when(even(q, r) == 0)
            def _():
                relay(q, r, near).wait_send()
                relay(q, r, mate).wait_send()

            for cp in c1(q, r):
                cp.wait_send()
            c2(q, r).wait_send()
            away, _, here = c3(q, r)

            @pl.when(here == 0)
            def _():
                away.wait_send()

            if q:
                z_copy(q, r).wait_send()
                back(q, r).wait_send()


def on_device(tokens, expert_ids, gate_weights, donor_group, gate_pieces, up_pieces, down_pieces):
    tok = tokens.reshape(128, D)
    ids = expert_ids.reshape(128, 2).T.astype(F32)
    wts = gate_weights.reshape(128, 2).T
    meta = jnp.concatenate([ids, wts, jnp.zeros((4, 128), F32)], axis=0)
    vmem, hbm = pltpu.VMEM, pl.ANY
    dma = pltpu.SemaphoreType.DMA
    mixed, landed = pl.pallas_call(
        layer,
        out_shape=(
            jax.ShapeDtypeStruct((128, D), BF),
            jax.ShapeDtypeStruct((3, SPAN, F), BF),
        ),
        in_specs=[
            pl.BlockSpec(memory_space=hbm),
            pl.BlockSpec(memory_space=vmem),
            pl.BlockSpec(memory_space=pltpu.SMEM),
            pl.BlockSpec(memory_space=hbm),
            pl.BlockSpec(memory_space=hbm),
            pl.BlockSpec(memory_space=hbm),
        ],
        out_specs=(pl.BlockSpec(memory_space=vmem), pl.BlockSpec(memory_space=vmem)),
        scratch_shapes=[
            vmem((256, D), BF),
            vmem((8, 128), F32),
            vmem((4 * CH, 256), BF),
            vmem((4 * CH, 256), BF),
            vmem((4 * CH, D), BF),
            vmem((3 * CH, D), BF),
            vmem((16 * CH, D), BF),
            vmem((D, F), BF),
            vmem((D, F), BF),
            vmem((D, F), BF),
            vmem((4 * CH, F), F32),
            vmem((4 * CH, F), F32),
            vmem((16 * CH, F), BF),
            vmem((16 * CH, D), BF),
            vmem((8 * CH, D), BF),
            vmem((4 * CH, D), BF),
            vmem((3 * CH, D), BF),
            vmem((4 * CH, D), BF),
            vmem((256, D), F32),
            vmem((128, D), BF),
            vmem((128, D), BF),
            vmem((12, SPAN, F), BF),
            vmem((3, SPAN, F), BF),
            vmem((3, SPAN, F), BF),
            dma((7,)),
            dma, dma,
            dma((K,)), dma((K,)),
            dma((6,)), dma((6,)),
            dma((16,)), dma((32,)), dma((32,)),
            dma((16,)), dma((16,)),
            dma((8,)), dma((8,)),
            dma((8,)), dma((8,)),
            dma((6,)), dma((6,)),
            dma((9,)), dma((9,)),
            dma, dma,
            dma((K,)), dma((K,)),
        ],
        compiler_params=pltpu.CompilerParams(
            collective_id=0, has_side_effects=True, vmem_limit_bytes=62 * 2**20
        ),
        cost_estimate=pl.CostEstimate(
            flops=8 * 10**9, bytes_accessed=10**7, transcendentals=4 * 10**5
        ),
    )(tok, meta, donor_group, gate_pieces[0], up_pieces[0], down_pieces[0])
    return mixed.reshape(2, 64, D), landed


def solution(mesh):
    in_specs = (
        P(None, ("grp", "ep"), None),
        P(None, ("grp", "ep"), None),
        P(None, ("grp", "ep"), None),
        P(),
        P(("grp", "ep"), None, None),
        P(("grp", "ep"), None, None),
        P(("grp", "ep"), None, None),
    )
    out_specs = (P(None, ("grp", "ep"), None), P(None, ("grp", "ep"), None))
    return jax.shard_map(
        on_device, mesh=mesh, in_specs=in_specs, out_specs=out_specs, check_vma=False
    )
```

```python
import jax
import jax.numpy as jnp
from jax import lax
from jax.experimental import pallas as pl
from jax.experimental.pallas import tpu as pltpu
from jax.sharding import PartitionSpec as P

MESH = pl.DeviceIdType.MESH
D = 3584
F = 256
CAP = 20
HALF = 40
CH = 80
K = 2
WIDE = D // K
TILE = 896
LEN = (32, 48)
OFF = (0, 32)
SPAN = 448
BF = jnp.bfloat16
F32 = jnp.float32


def rows(index, size=CH):
    return pl.ds(pl.multiple_of(index * size, 16), size)


def layer(
    tok_ref, meta_ref, donor_ref, gate_ref, up_ref, down_ref, mixed_ref, landed_ref,
    tok_all, meta_all, onehot, weight_t, pack, zin, xin, gw, uw, dw, gacc, uacc, hid,
    part, c1buf, c2buf, zout, home, acc, ex_send, ex_recv, cand, lsend, lrecv,
    load_sem, m_send, m_recv, t_send, t_recv, z_send, z_recv, x_send, x_recv, r_send,
    c1_send, c1_recv, c2_send, c2_recv, c3_send, zo_recv, b_send, b_recv,
    y_send, y_recv, l_send, l_recv, e_send, e_recv,
):
    grp = lax.axis_index("grp")
    ep = lax.axis_index("ep")
    y, zl = grp // 2, grp % 2
    z, x, c = ep // 8, (ep // 2) % 4, ep % 2
    pair = x // 2
    mate = x + 1 - 2 * (x % 2)
    cross = (x + 2) % 4
    near = 3 - x
    serve = 1 - (pair + c) % 2

    def at(zz, xx, cc):
        return (grp, zz * 8 + xx * 2 + cc)

    sibling = at(z, x, 1 - c)

    def ygroup(d):
        return (((y + d) % 4) * 2 + zl, ep)

    partner = (y * 2 + 1 - zl, ep)

    def remote(src, dst, send, recv, target):
        return pltpu.make_async_remote_copy(
            src_ref=src, dst_ref=dst, send_sem=send, recv_sem=recv,
            device_id=target, device_id_type=MESH,
        )

    def arrived(ref, sem):
        pltpu.make_async_copy(ref, ref, sem).wait()

    def piece(k):
        return pl.ds(k * WIDE, WIDE)

    def chunk(q, r, sides=1):
        return pl.ds(sides * (q * CH + OFF[r]), sides * LEN[r])

    def side(q, r, sides, i):
        base = sides * (q * CH + OFF[r])
        return pl.ds(pl.multiple_of(base + i * LEN[r], 16), LEN[r])

    pieces = (gate_ref, up_ref, down_ref)
    loads = [
        pltpu.make_async_copy(tok_ref, tok_all.at[pl.ds(0, 128)], load_sem.at[0]),
        pltpu.make_async_copy(gate_ref, gw, load_sem.at[1]),
        pltpu.make_async_copy(up_ref, uw, load_sem.at[2]),
        pltpu.make_async_copy(down_ref, dw, load_sem.at[3]),
    ] + [
        pltpu.make_async_copy(pieces[j].at[pl.ds(0, SPAN)], cand.at[j], load_sem.at[4 + j])
        for j in range(3)
    ]
    for cp in loads:
        cp.start()

    barrier = pltpu.get_barrier_semaphore()
    greeted = [at(z, x, 1 - c)]
    greeted += [at(z, (x + i) % 4, c) for i in range(1, 4)]
    greeted += [at(z, (x + i) % 4, 1 - c) for i in range(1, 4)]
    greeted += [at((z + i) % 4, x, c) for i in range(1, 4)]
    greeted += [ygroup(i) for i in range(1, 4)]
    greeted += [partner]
    for target in greeted:
        pl.semaphore_signal(barrier, inc=1, device_id=target, device_id_type=MESH)
    pl.semaphore_wait(barrier, len(greeted))

    sib_meta = remote(meta_ref, meta_all, m_send, m_recv, sibling)
    sib_meta.start()

    def sib_tok(k):
        return remote(
            tok_ref.at[:, piece(k)], tok_all.at[pl.ds(128, 128), piece(k)],
            t_send.at[k], t_recv.at[k], sibling,
        )

    for k in range(K):
        sib_tok(k).start()
    y_copies = []
    for n, d in enumerate((1, 3, 2)):
        for j in range(3):
            cp = remote(
                pieces[j].at[pl.ds(0, SPAN)], cand.at[((4 - d) % 4) * 3 + j],
                y_send.at[n * 3 + j], y_recv.at[(d - 1) * 3 + j], ygroup(d),
            )
            cp.start()
            y_copies.append(cp)

    sib_meta.wait_recv()
    row8 = lax.broadcasted_iota(jnp.int32, (8, 128), 0)
    lane8 = lax.broadcasted_iota(jnp.int32, (8, 128), 1)
    expert = (2 * ((row8 + z) % 4) + c).astype(F32)
    first = lax.broadcasted_iota(jnp.int32, (128, 128), 0)
    second = lax.broadcasted_iota(jnp.int32, (128, 128), 1)
    before = jnp.where((first < second) & (first // 64 == second // 64), 1.0, 0.0).astype(BF)
    slot = lax.broadcasted_iota(jnp.int32, (CH, 128), 0).astype(F32)
    for h, meta in enumerate((meta_ref, meta_all)):
        id0, id1 = meta[0:1, :], meta[1:2, :]
        w0, w1 = meta[2:3, :], meta[3:4, :]
        hit0, hit1 = expert == id0, expert == id1
        named = jnp.where(hit0 | hit1, 1.0, 0.0)
        rank = jnp.dot(named.astype(BF), before, preferred_element_type=F32)
        place = rank + jnp.where(lane8 >= 64, float(CAP), 0.0) + float(HALF * h)
        place = jnp.where(named > 0.0, place, -1.0)
        weight = jnp.where(hit0, w0, jnp.where(hit1, w1, 0.0))
        for d in range(4):
            match = place[d : d + 1, :] == slot
            here = (pl.ds(d * CH, CH), pl.ds(h * 128, 128))
            onehot[here] = jnp.where(match, 1.0, 0.0).astype(BF)
            weight_t[here] = jnp.where(match, weight[d : d + 1, :], 0.0).astype(BF)

    loads[0].wait()

    def tiles(body, start=0, size=D):
        def step(i, carry):
            body(pl.ds(pl.multiple_of(start + i * TILE, 128), TILE))
            return carry

        lax.fori_loop(0, size // TILE, step, 0)

    def pack_chunk(d, k):
        def body(cols):
            pack[pl.ds(d * CH, CH), cols] = jnp.dot(
                onehot[pl.ds(d * CH, CH), :], tok_all[:, cols], preferred_element_type=F32
            ).astype(BF)

        tiles(body, k * WIDE, WIDE)

    def z_copy(d, r):
        n = (d - 1) * 2 + r
        return remote(
            pack.at[chunk(d, r)], zin.at[chunk(d - 1, r)],
            z_send.at[n], z_recv.at[n], at((z + d) % 4, x, c),
        )

    def fan(q, r):
        src = pack.at[chunk(0, r)]
        if q:
            src = zin.at[chunk(q - 1, r)]
        dst = xin.at[side(q, r, 4, x)]
        f = (q // 2 + x + r) % 2
        n = q * 2 + r
        recv = x_recv.at[n * 4 + x]
        t0 = at(z, serve * mate + (1 - serve) * near, f)
        return (
            remote(src, dst, x_send.at[n * 2], recv, t0),
            remote(src, dst, x_send.at[n * 2 + 1], recv, sibling),
            pltpu.make_async_copy(src, dst, recv),
            remote(src, dst, x_send.at[n * 2 + 1], recv, at(z, cross, f)),
        )

    def fan_start(q, r):
        away, over, local, beyond = fan(q, r)
        away.start()

        @pl.when(serve == 1)
        def _():
            over.start()
            local.start()

        @pl.when(serve == 0)
        def _():
            beyond.start()

    def even(q, r):
        return 1 - (x + c + q // 2 + r) % 2

    def x_wait(q, r, xs):
        arrived(xin.at[side(q, r, 4, xs)], x_recv.at[(q * 2 + r) * 4 + xs])

    def relay(q, r, xs):
        ref = xin.at[side(q, r, 4, xs)]
        n = (q * 2 + r) * 4 + xs
        return remote(ref, ref, r_send.at[n], x_recv.at[n], sibling)

    def relay_near(q, r):
        @pl.when(even(q, r) == 0)
        def _():
            x_wait(q, r, near)
            relay(q, r, near).start()

    def relay_rest(q, r):
        @pl.when(even(q, r) == 0)
        def _():
            x_wait(q, r, mate)
            relay(q, r, mate).start()

        @pl.when(even(q, r) == 1)
        def _():
            x_wait(q, r, cross)
            relay(q, r, cross).start()

    def up(q, r):
        @pl.when(even(q, r) == 0)
        def _():
            x_wait(q, r, cross)

        @pl.when(even(q, r) == 1)
        def _():
            x_wait(q, r, near)
            x_wait(q, r, mate)

        x_wait(q, r, x)
        o = chunk(q, r, 4)
        s = pl.ds(0, 4 * LEN[r])
        gacc[s, :] = jnp.zeros((4 * LEN[r], F), F32)
        uacc[s, :] = jnp.zeros((4 * LEN[r], F), F32)

        def body(cols):
            a = xin[o, cols]
            gacc[s, :] += jnp.dot(a, gw[cols, :], preferred_element_type=F32)
            uacc[s, :] += jnp.dot(a, uw[cols, :], preferred_element_type=F32)

        tiles(body)
        g = gacc[s, :]
        hid[o, :] = (g / (1.0 + jnp.exp(-g)) * uacc[s, :]).astype(BF)

    def keep_of(q, r, own):
        u = even(q, r) if own else 1 - even(q, r)
        return u * x + (1 - u) * near

    def send_of(q, r, own):
        u = even(q, r) if own else 1 - even(q, r)
        return u * cross + (1 - u) * mate

    def c1(q, r):
        n = (q * 2 + r) * 2
        return (
            remote(
                part.at[side(q, r, 4, send_of(q, r, False))],
                c1buf.at[side(q, r, 2, 1)],
                c1_send.at[n + 1], c1_recv.at[n + 1], sibling,
            ),
            remote(
                part.at[side(q, r, 4, keep_of(q, r, False))],
                c1buf.at[side(q, r, 2, 0)],
                c1_send.at[n], c1_recv.at[n], sibling,
            ),
        )

    def down(q, r):
        o = chunk(q, r, 4)

        def body(cols):
            part[o, cols] = lax.dot_general(
                hid[o, :], dw[cols, :], (((1,), (1,)), ((), ())), preferred_element_type=F32
            ).astype(BF)

        tiles(body)
        for cp in c1(q, r):
            cp.start()

    def c2(q, r):
        n = q * 2 + r
        return remote(
            part.at[side(q, r, 4, send_of(q, r, True))],
            c2buf.at[chunk(q, r)],
            c2_send.at[n], c2_recv.at[n], at(z, mate, c),
        )

    def add_rows(target, buffers, count):
        def step(i, carry):
            total = part[pl.ds(pl.multiple_of(target.start + i * 16, 16), 16), :].astype(F32)
            for buf, other in buffers:
                total += buf[pl.ds(pl.multiple_of(other.start + i * 16, 16), 16), :].astype(F32)
            part[pl.ds(pl.multiple_of(target.start + i * 16, 16), 16), :] = total.astype(BF)
            return carry

        lax.fori_loop(0, count // 16, step, 0)

    def c2_start(q, r):
        c1(q, r)[0].wait_recv()
        add_rows(side(q, r, 4, send_of(q, r, True)), [(c1buf, side(q, r, 2, 1))], LEN[r])
        c2(q, r).start()

    def c3(q, r):
        src = part.at[side(q, r, 4, keep_of(q, r, True))]
        dst = home.at[chunk(0, r)]
        if q:
            dst = zout.at[chunk(q - 1, r)]
        u = even(q, r)
        n = q * 2 + r
        return (
            remote(src, dst, c3_send.at[n], zo_recv.at[n], at(z, u * x + (1 - u) * near, pair)),
            pltpu.make_async_copy(src, dst, zo_recv.at[n]),
            u * serve,
        )

    def c3_start(q, r):
        c1(q, r)[1].wait_recv()
        c2(q, r).wait_recv()
        add_rows(
            side(q, r, 4, keep_of(q, r, True)),
            [(c1buf, side(q, r, 2, 0)), (c2buf, chunk(q, r))],
            LEN[r],
        )
        away, local, here = c3(q, r)

        @pl.when(here == 1)
        def _():
            local.start()

        @pl.when(here == 0)
        def _():
            away.start()

    def back(q, r):
        n = (q - 1) * 2 + r
        return remote(
            zout.at[chunk(q - 1, r)], home.at[chunk(q, r)],
            b_send.at[n], b_recv.at[n], at((z + 4 - q) % 4, x, c),
        )

    def back_start(q, r):
        arrived(zout.at[chunk(q - 1, r)], zo_recv.at[q * 2 + r])
        back(q, r).start()

    def swap(k):
        return remote(
            ex_send.at[:, piece(k)], ex_recv.at[:, piece(k)], e_send.at[k], e_recv.at[k], sibling
        )

    def mix(q, parts, start=False, last=False):
        for r in parts:
            if q:
                back(q, r).wait_recv()
            else:
                arrived(home.at[chunk(0, r)], zo_recv.at[r])
        s = chunk(q, 0) if len(parts) == 1 else pl.ds(q * CH, CH)
        if parts == (1,):
            s = chunk(q, 1)

        def body(cols):
            value = lax.dot_general(
                weight_t[s, :], home[s, cols], (((0,), (0,)), ((), ())),
                preferred_element_type=F32,
            )
            if not start:
                value += acc[:, cols]
            if last:
                acc[pl.ds(0, 128), cols] = value[:128]
                ex_send[:, cols] = value[128:].astype(BF)
            else:
                acc[:, cols] = value

        for k in range(K):
            tiles(body, k * WIDE, WIDE)
            if last:
                swap(k).start()

    def join(k):
        swap(k).wait()

        def body(cols):
            mixed_ref[:, cols] = (
                acc[pl.ds(0, 128), cols] + ex_recv[:, cols].astype(F32)
            ).astype(BF)

        tiles(body, k * WIDE, WIDE)

    def pick():
        for j in range(3):
            loads[4 + j].wait()
        for cp in y_copies:
            cp.wait_send()
        for d in (1, 2, 3):
            for j in range(3):
                arrived(cand.at[((4 - d) % 4) * 3 + j], y_recv.at[(d - 1) * 3 + j])
        asked = donor_ref[y * 2 + 1 - zl, ep]
        asked_y = (asked // 2 + 4 - y) % 4
        for j in range(3):
            lsend[j] = cand[asked_y * 3 + j]

    l_copy = remote(lsend, lrecv, l_send, l_recv, partner)

    def land():
        l_copy.wait()
        wanted = donor_ref[grp, ep]
        wanted_y = (wanted // 2 + 4 - y) % 4
        wanted_z = wanted % 2
        from_here = jnp.full((SPAN, F), wanted_z, jnp.int32) == zl
        for j in range(3):
            close = cand[wanted_y * 3 + j].astype(F32)
            far = lrecv[j].astype(F32)
            landed_ref[j] = jnp.where(from_here, close, far).astype(BF)

    sib_tok(0).wait_recv()
    pack_chunk(1, 0)
    pack_chunk(3, 0)
    sib_tok(1).wait_recv()
    pack_chunk(1, 1)
    z_copy(1, 0).start()
    pack_chunk(3, 1)
    z_copy(3, 0).start()
    pack_chunk(0, 0)
    pack_chunk(0, 1)
    fan_start(0, 0)
    fan_start(0, 1)
    pack_chunk(2, 0)
    pack_chunk(2, 1)
    z_copy(2, 0).start()
    z_copy(1, 1).start()
    z_copy(3, 1).start()
    z_copy(2, 1).start()
    relay_near(0, 0)
    for n in (1, 2, 3):
        loads[n].wait()
    relay_rest(0, 0)
    up(0, 0)
    down(0, 0)
    relay_near(0, 1)
    relay_rest(0, 1)
    z_copy(1, 0).wait_recv()
    fan_start(1, 0)
    z_copy(3, 0).wait_recv()
    fan_start(3, 0)
    up(0, 1)
    down(0, 1)
    relay_near(1, 0)
    relay_near(3, 0)
    z_copy(2, 0).wait_recv()
    fan_start(2, 0)
    relay_rest(1, 0)
    relay_rest(3, 0)
    up(1, 0)
    down(1, 0)
    c2_start(1, 0)
    up(3, 0)
    down(3, 0)
    c2_start(3, 0)
    z_copy(1, 1).wait_recv()
    fan_start(1, 1)
    z_copy(3, 1).wait_recv()
    fan_start(3, 1)
    relay_near(2, 0)
    relay_rest(2, 0)
    up(2, 0)
    down(2, 0)
    c2_start(2, 0)
    pick()
    z_copy(2, 1).wait_recv()
    fan_start(2, 1)
    l_copy.start()
    c3_start(1, 0)
    c3_start(3, 0)
    relay_near(1, 1)
    relay_near(3, 1)
    back_start(1, 0)
    back_start(3, 0)
    relay_rest(1, 1)
    relay_rest(3, 1)
    up(1, 1)
    down(1, 1)
    c2_start(1, 1)
    up(3, 1)
    down(3, 1)
    c2_start(3, 1)
    c3_start(2, 0)
    relay_near(2, 1)
    relay_rest(2, 1)
    back_start(2, 0)
    up(2, 1)
    down(2, 1)
    c2_start(2, 1)
    c2_start(0, 0)
    c2_start(0, 1)
    c3_start(1, 1)
    c3_start(3, 1)
    back_start(1, 1)
    back_start(3, 1)
    mix(1, (0,), start=True)
    c3_start(2, 1)
    mix(3, (0,))
    back_start(2, 1)
    mix(2, (0,))
    c3_start(0, 0)
    c3_start(0, 1)
    land()
    mix(1, (1,))
    mix(3, (1,))
    mix(2, (1,))
    mix(0, (0,))
    mix(0, (1,), last=True)
    join(0)
    join(1)
    sib_meta.wait_send()
    for k in range(K):
        sib_tok(k).wait_send()
    for q in range(4):
        for r in range(2):
            away, over, _, beyond = fan(q, r)
            away.wait_send()

            @pl.when(serve == 1)
            def _():
                over.wait_send()

            @pl.when(serve == 0)
            def _():
                beyond.wait_send()

            @pl.when(even(q, r) == 1)
            def _():
                relay(q, r, cross).wait_send()

            @pl.when(even(q, r) == 0)
            def _():
                relay(q, r, near).wait_send()
                relay(q, r, mate).wait_send()

            for cp in c1(q, r):
                cp.wait_send()
            c2(q, r).wait_send()
            away, _, here = c3(q, r)

            @pl.when(here == 0)
            def _():
                away.wait_send()

            if q:
                z_copy(q, r).wait_send()
                back(q, r).wait_send()


def on_device(tokens, expert_ids, gate_weights, donor_group, gate_pieces, up_pieces, down_pieces):
    tok = tokens.reshape(128, D)
    ids = expert_ids.reshape(128, 2).T.astype(F32)
    wts = gate_weights.reshape(128, 2).T
    meta = jnp.concatenate([ids, wts, jnp.zeros((4, 128), F32)], axis=0)
    vmem, hbm = pltpu.VMEM, pl.ANY
    dma = pltpu.SemaphoreType.DMA
    mixed, landed = pl.pallas_call(
        layer,
        out_shape=(
            jax.ShapeDtypeStruct((128, D), BF),
            jax.ShapeDtypeStruct((3, SPAN, F), BF),
        ),
        in_specs=[
            pl.BlockSpec(memory_space=hbm),
            pl.BlockSpec(memory_space=vmem),
            pl.BlockSpec(memory_space=pltpu.SMEM),
            pl.BlockSpec(memory_space=hbm),
            pl.BlockSpec(memory_space=hbm),
            pl.BlockSpec(memory_space=hbm),
        ],
        out_specs=(pl.BlockSpec(memory_space=vmem), pl.BlockSpec(memory_space=vmem)),
        scratch_shapes=[
            vmem((256, D), BF),
            vmem((8, 128), F32),
            vmem((4 * CH, 256), BF),
            vmem((4 * CH, 256), BF),
            vmem((4 * CH, D), BF),
            vmem((3 * CH, D), BF),
            vmem((16 * CH, D), BF),
            vmem((D, F), BF),
            vmem((D, F), BF),
            vmem((D, F), BF),
            vmem((4 * CH, F), F32),
            vmem((4 * CH, F), F32),
            vmem((16 * CH, F), BF),
            vmem((16 * CH, D), BF),
            vmem((8 * CH, D), BF),
            vmem((4 * CH, D), BF),
            vmem((3 * CH, D), BF),
            vmem((4 * CH, D), BF),
            vmem((256, D), F32),
            vmem((128, D), BF),
            vmem((128, D), BF),
            vmem((12, SPAN, F), BF),
            vmem((3, SPAN, F), BF),
            vmem((3, SPAN, F), BF),
            dma((7,)),
            dma, dma,
            dma((K,)), dma((K,)),
            dma((6,)), dma((6,)),
            dma((16,)), dma((32,)), dma((32,)),
            dma((16,)), dma((16,)),
            dma((8,)), dma((8,)),
            dma((8,)), dma((8,)),
            dma((6,)), dma((6,)),
            dma((9,)), dma((9,)),
            dma, dma,
            dma((K,)), dma((K,)),
        ],
        compiler_params=pltpu.CompilerParams(
            collective_id=0, has_side_effects=True, vmem_limit_bytes=62 * 2**20
        ),
        cost_estimate=pl.CostEstimate(
            flops=8 * 10**9, bytes_accessed=10**7, transcendentals=4 * 10**5
        ),
    )(tok, meta, donor_group, gate_pieces[0], up_pieces[0], down_pieces[0])
    return mixed.reshape(2, 64, D), landed


def solution(mesh):
    in_specs = (
        P(None, ("grp", "ep"), None),
        P(None, ("grp", "ep"), None),
        P(None, ("grp", "ep"), None),
        P(),
        P(("grp", "ep"), None, None),
        P(("grp", "ep"), None, None),
        P(("grp", "ep"), None, None),
    )
    out_specs = (P(None, ("grp", "ep"), None), P(None, ("grp", "ep"), None))
    return jax.shard_map(
        on_device, mesh=mesh, in_specs=in_specs, out_specs=out_specs, check_vma=False
    )
```

```python
import jax
import jax.numpy as jnp
from jax import lax
from jax.experimental import pallas as pl
from jax.experimental.pallas import tpu as pltpu
from jax.sharding import PartitionSpec as P

MESH = pl.DeviceIdType.MESH
D = 3584
F = 256
CAP = 20
HALF = 40
CH = 80
K = 2
WIDE = D // K
TILE = 896
LEN = (32, 48)
OFF = (0, 32)
SPAN = 448
BF = jnp.bfloat16
F32 = jnp.float32


def rows(index, size=CH):
    return pl.ds(pl.multiple_of(index * size, 16), size)


def layer(
    tok_ref, meta_ref, donor_ref, gate_ref, up_ref, down_ref, mixed_ref, landed_ref,
    tok_all, meta_all, onehot, weight_t, pack, zin, xin, gw, uw, dw, gacc, uacc, hid,
    part, c1buf, c2buf, zout, home, acc, ex_send, ex_recv, cand, lsend, lrecv,
    load_sem, m_send, m_recv, t_send, t_recv, z_send, z_recv, x_send, x_recv, r_send,
    c1_send, c1_recv, c2_send, c2_recv, c3_send, zo_recv, b_send, b_recv,
    y_send, y_recv, l_send, l_recv, e_send, e_recv,
):
    grp = lax.axis_index("grp")
    ep = lax.axis_index("ep")
    y, zl = grp // 2, grp % 2
    z, x, c = ep // 8, (ep // 2) % 4, ep % 2
    pair = x // 2
    mate = x + 1 - 2 * (x % 2)
    cross = (x + 2) % 4
    near = 3 - x
    serve = 1 - (pair + c) % 2

    def at(zz, xx, cc):
        return (grp, zz * 8 + xx * 2 + cc)

    sibling = at(z, x, 1 - c)

    def ygroup(d):
        return (((y + d) % 4) * 2 + zl, ep)

    partner = (y * 2 + 1 - zl, ep)

    def remote(src, dst, send, recv, target):
        return pltpu.make_async_remote_copy(
            src_ref=src, dst_ref=dst, send_sem=send, recv_sem=recv,
            device_id=target, device_id_type=MESH,
        )

    def arrived(ref, sem):
        pltpu.make_async_copy(ref, ref, sem).wait()

    def piece(k):
        return pl.ds(k * WIDE, WIDE)

    def chunk(q, r, sides=1):
        return pl.ds(sides * (q * CH + OFF[r]), sides * LEN[r])

    def side(q, r, sides, i):
        base = sides * (q * CH + OFF[r])
        return pl.ds(pl.multiple_of(base + i * LEN[r], 16), LEN[r])

    pieces = (gate_ref, up_ref, down_ref)
    loads = [
        pltpu.make_async_copy(tok_ref, tok_all.at[pl.ds(0, 128)], load_sem.at[0]),
        pltpu.make_async_copy(gate_ref, gw, load_sem.at[1]),
        pltpu.make_async_copy(up_ref, uw, load_sem.at[2]),
        pltpu.make_async_copy(down_ref, dw, load_sem.at[3]),
    ] + [
        pltpu.make_async_copy(pieces[j].at[pl.ds(0, SPAN)], cand.at[j], load_sem.at[4 + j])
        for j in range(3)
    ]
    for cp in loads:
        cp.start()

    barrier = pltpu.get_barrier_semaphore()
    greeted = [at(z, x, 1 - c)]
    greeted += [at(z, (x + i) % 4, c) for i in range(1, 4)]
    greeted += [at(z, (x + i) % 4, 1 - c) for i in range(1, 4)]
    greeted += [at((z + i) % 4, x, c) for i in range(1, 4)]
    greeted += [ygroup(i) for i in range(1, 4)]
    greeted += [partner]
    for target in greeted:
        pl.semaphore_signal(barrier, inc=1, device_id=target, device_id_type=MESH)
    pl.semaphore_wait(barrier, len(greeted))

    sib_meta = remote(meta_ref, meta_all, m_send, m_recv, sibling)
    sib_meta.start()

    def sib_tok(k):
        return remote(
            tok_ref.at[:, piece(k)], tok_all.at[pl.ds(128, 128), piece(k)],
            t_send.at[k], t_recv.at[k], sibling,
        )

    for k in range(K):
        sib_tok(k).start()
    y_copies = []
    for n, d in enumerate((1, 3, 2)):
        for j in range(3):
            cp = remote(
                pieces[j].at[pl.ds(0, SPAN)], cand.at[((4 - d) % 4) * 3 + j],
                y_send.at[n * 3 + j], y_recv.at[(d - 1) * 3 + j], ygroup(d),
            )
            cp.start()
            y_copies.append(cp)

    sib_meta.wait_recv()
    row8 = lax.broadcasted_iota(jnp.int32, (8, 128), 0)
    lane8 = lax.broadcasted_iota(jnp.int32, (8, 128), 1)
    expert = (2 * ((row8 + z) % 4) + c).astype(F32)
    first = lax.broadcasted_iota(jnp.int32, (128, 128), 0)
    second = lax.broadcasted_iota(jnp.int32, (128, 128), 1)
    before = jnp.where((first < second) & (first // 64 == second // 64), 1.0, 0.0).astype(BF)
    slot = lax.broadcasted_iota(jnp.int32, (CH, 128), 0).astype(F32)
    for h, meta in enumerate((meta_ref, meta_all)):
        id0, id1 = meta[0:1, :], meta[1:2, :]
        w0, w1 = meta[2:3, :], meta[3:4, :]
        hit0, hit1 = expert == id0, expert == id1
        named = jnp.where(hit0 | hit1, 1.0, 0.0)
        rank = jnp.dot(named.astype(BF), before, preferred_element_type=F32)
        place = rank + jnp.where(lane8 >= 64, float(CAP), 0.0) + float(HALF * h)
        place = jnp.where(named > 0.0, place, -1.0)
        weight = jnp.where(hit0, w0, jnp.where(hit1, w1, 0.0))
        for d in range(4):
            match = place[d : d + 1, :] == slot
            here = (pl.ds(d * CH, CH), pl.ds(h * 128, 128))
            onehot[here] = jnp.where(match, 1.0, 0.0).astype(BF)
            weight_t[here] = jnp.where(match, weight[d : d + 1, :], 0.0).astype(BF)

    loads[0].wait()

    def tiles(body, start=0, size=D):
        def step(i, carry):
            body(pl.ds(pl.multiple_of(start + i * TILE, 128), TILE))
            return carry

        lax.fori_loop(0, size // TILE, step, 0)

    def pack_chunk(d, k):
        def body(cols):
            pack[pl.ds(d * CH, CH), cols] = jnp.dot(
                onehot[pl.ds(d * CH, CH), :], tok_all[:, cols], preferred_element_type=F32
            ).astype(BF)

        tiles(body, k * WIDE, WIDE)

    def z_copy(d, r):
        n = (d - 1) * 2 + r
        return remote(
            pack.at[chunk(d, r)], zin.at[chunk(d - 1, r)],
            z_send.at[n], z_recv.at[n], at((z + d) % 4, x, c),
        )

    def fan(q, r):
        src = pack.at[chunk(0, r)]
        if q:
            src = zin.at[chunk(q - 1, r)]
        dst = xin.at[side(q, r, 4, x)]
        f = (q + x + r) % 2
        n = q * 2 + r
        recv = x_recv.at[n * 4 + x]
        t0 = at(z, serve * mate + (1 - serve) * near, f)
        return (
            remote(src, dst, x_send.at[n * 2], recv, t0),
            remote(src, dst, x_send.at[n * 2 + 1], recv, sibling),
            pltpu.make_async_copy(src, dst, recv),
            remote(src, dst, x_send.at[n * 2 + 1], recv, at(z, cross, f)),
        )

    def fan_start(q, r):
        away, over, local, beyond = fan(q, r)
        away.start()

        @pl.when(serve == 1)
        def _():
            over.start()
            local.start()

        @pl.when(serve == 0)
        def _():
            beyond.start()

    def even(q, r):
        return 1 - (x + c + q + r) % 2

    def x_wait(q, r, xs):
        arrived(xin.at[side(q, r, 4, xs)], x_recv.at[(q * 2 + r) * 4 + xs])

    def relay(q, r, xs):
        ref = xin.at[side(q, r, 4, xs)]
        n = (q * 2 + r) * 4 + xs
        return remote(ref, ref, r_send.at[n], x_recv.at[n], sibling)

    def relay_near(q, r):
        @pl.when(even(q, r) == 0)
        def _():
            x_wait(q, r, near)
            relay(q, r, near).start()

    def relay_rest(q, r):
        @pl.when(even(q, r) == 0)
        def _():
            x_wait(q, r, mate)
            relay(q, r, mate).start()

        @pl.when(even(q, r) == 1)
        def _():
            x_wait(q, r, cross)
            relay(q, r, cross).start()

    def up(q, r):
        @pl.when(even(q, r) == 0)
        def _():
            x_wait(q, r, cross)

        @pl.when(even(q, r) == 1)
        def _():
            x_wait(q, r, near)
            x_wait(q, r, mate)

        x_wait(q, r, x)
        o = chunk(q, r, 4)
        s = pl.ds(0, 4 * LEN[r])
        gacc[s, :] = jnp.zeros((4 * LEN[r], F), F32)
        uacc[s, :] = jnp.zeros((4 * LEN[r], F), F32)

        def body(cols):
            a = xin[o, cols]
            gacc[s, :] += jnp.dot(a, gw[cols, :], preferred_element_type=F32)
            uacc[s, :] += jnp.dot(a, uw[cols, :], preferred_element_type=F32)

        tiles(body)
        g = gacc[s, :]
        hid[o, :] = (g / (1.0 + jnp.exp(-g)) * uacc[s, :]).astype(BF)

    def keep_of(q, r, own):
        u = even(q, r) if own else 1 - even(q, r)
        return u * x + (1 - u) * near

    def send_of(q, r, own):
        u = even(q, r) if own else 1 - even(q, r)
        return u * cross + (1 - u) * mate

    def c1(q, r):
        n = (q * 2 + r) * 2
        return (
            remote(
                part.at[side(q, r, 4, send_of(q, r, False))],
                c1buf.at[side(q, r, 2, 1)],
                c1_send.at[n + 1], c1_recv.at[n + 1], sibling,
            ),
            remote(
                part.at[side(q, r, 4, keep_of(q, r, False))],
                c1buf.at[side(q, r, 2, 0)],
                c1_send.at[n], c1_recv.at[n], sibling,
            ),
        )

    def down(q, r):
        o = chunk(q, r, 4)

        def body(cols):
            part[o, cols] = lax.dot_general(
                hid[o, :], dw[cols, :], (((1,), (1,)), ((), ())), preferred_element_type=F32
            ).astype(BF)

        tiles(body)
        for cp in c1(q, r):
            cp.start()

    def c2(q, r):
        n = q * 2 + r
        return remote(
            part.at[side(q, r, 4, send_of(q, r, True))],
            c2buf.at[chunk(q, r)],
            c2_send.at[n], c2_recv.at[n], at(z, mate, c),
        )

    def add_rows(target, buffers, count):
        def step(i, carry):
            total = part[pl.ds(pl.multiple_of(target.start + i * 16, 16), 16), :].astype(F32)
            for buf, other in buffers:
                total += buf[pl.ds(pl.multiple_of(other.start + i * 16, 16), 16), :].astype(F32)
            part[pl.ds(pl.multiple_of(target.start + i * 16, 16), 16), :] = total.astype(BF)
            return carry

        lax.fori_loop(0, count // 16, step, 0)

    def c2_start(q, r):
        c1(q, r)[0].wait_recv()
        add_rows(side(q, r, 4, send_of(q, r, True)), [(c1buf, side(q, r, 2, 1))], LEN[r])
        c2(q, r).start()

    def c3(q, r):
        src = part.at[side(q, r, 4, keep_of(q, r, True))]
        dst = home.at[chunk(0, r)]
        if q:
            dst = zout.at[chunk(q - 1, r)]
        u = even(q, r)
        n = q * 2 + r
        return (
            remote(src, dst, c3_send.at[n], zo_recv.at[n], at(z, u * x + (1 - u) * near, pair)),
            pltpu.make_async_copy(src, dst, zo_recv.at[n]),
            u * serve,
        )

    def c3_start(q, r):
        c1(q, r)[1].wait_recv()
        c2(q, r).wait_recv()
        add_rows(
            side(q, r, 4, keep_of(q, r, True)),
            [(c1buf, side(q, r, 2, 0)), (c2buf, chunk(q, r))],
            LEN[r],
        )
        away, local, here = c3(q, r)

        @pl.when(here == 1)
        def _():
            local.start()

        @pl.when(here == 0)
        def _():
            away.start()

    def back(q, r):
        n = (q - 1) * 2 + r
        return remote(
            zout.at[chunk(q - 1, r)], home.at[chunk(q, r)],
            b_send.at[n], b_recv.at[n], at((z + 4 - q) % 4, x, c),
        )

    def back_start(q, r):
        arrived(zout.at[chunk(q - 1, r)], zo_recv.at[q * 2 + r])
        back(q, r).start()

    def swap(k):
        return remote(
            ex_send.at[:, piece(k)], ex_recv.at[:, piece(k)], e_send.at[k], e_recv.at[k], sibling
        )

    def mix(q, parts, start=False, last=False):
        for r in parts:
            if q:
                back(q, r).wait_recv()
            else:
                arrived(home.at[chunk(0, r)], zo_recv.at[r])
        s = chunk(q, 0) if len(parts) == 1 else pl.ds(q * CH, CH)
        if parts == (1,):
            s = chunk(q, 1)

        def body(cols):
            value = lax.dot_general(
                weight_t[s, :], home[s, cols], (((0,), (0,)), ((), ())),
                preferred_element_type=F32,
            )
            if not start:
                value += acc[:, cols]
            if last:
                acc[pl.ds(0, 128), cols] = value[:128]
                ex_send[:, cols] = value[128:].astype(BF)
            else:
                acc[:, cols] = value

        for k in range(K):
            tiles(body, k * WIDE, WIDE)
            if last:
                swap(k).start()

    def join(k):
        swap(k).wait()

        def body(cols):
            mixed_ref[:, cols] = (
                acc[pl.ds(0, 128), cols] + ex_recv[:, cols].astype(F32)
            ).astype(BF)

        tiles(body, k * WIDE, WIDE)

    def pick():
        for j in range(3):
            loads[4 + j].wait()
        for cp in y_copies:
            cp.wait_send()
        for d in (1, 2, 3):
            for j in range(3):
                arrived(cand.at[((4 - d) % 4) * 3 + j], y_recv.at[(d - 1) * 3 + j])
        asked = donor_ref[y * 2 + 1 - zl, ep]
        asked_y = (asked // 2 + 4 - y) % 4
        for j in range(3):
            lsend[j] = cand[asked_y * 3 + j]

    l_copy = remote(lsend, lrecv, l_send, l_recv, partner)

    def land():
        l_copy.wait()
        wanted = donor_ref[grp, ep]
        wanted_y = (wanted // 2 + 4 - y) % 4
        wanted_z = wanted % 2
        from_here = jnp.full((SPAN, F), wanted_z, jnp.int32) == zl
        for j in range(3):
            close = cand[wanted_y * 3 + j].astype(F32)
            far = lrecv[j].astype(F32)
            landed_ref[j] = jnp.where(from_here, close, far).astype(BF)

    sib_tok(0).wait_recv()
    pack_chunk(1, 0)
    pack_chunk(3, 0)
    sib_tok(1).wait_recv()
    pack_chunk(1, 1)
    z_copy(1, 0).start()
    pack_chunk(3, 1)
    z_copy(3, 0).start()
    pack_chunk(0, 0)
    pack_chunk(0, 1)
    fan_start(0, 0)
    fan_start(0, 1)
    pack_chunk(2, 0)
    pack_chunk(2, 1)
    z_copy(2, 0).start()
    z_copy(1, 1).start()
    z_copy(3, 1).start()
    z_copy(2, 1).start()
    relay_near(0, 0)
    for n in (1, 2, 3):
        loads[n].wait()
    relay_rest(0, 0)
    up(0, 0)
    down(0, 0)
    relay_near(0, 1)
    relay_rest(0, 1)
    z_copy(1, 0).wait_recv()
    fan_start(1, 0)
    z_copy(3, 0).wait_recv()
    fan_start(3, 0)
    up(0, 1)
    down(0, 1)
    relay_near(1, 0)
    relay_near(3, 0)
    z_copy(2, 0).wait_recv()
    fan_start(2, 0)
    relay_rest(1, 0)
    relay_rest(3, 0)
    up(1, 0)
    down(1, 0)
    c2_start(1, 0)
    up(3, 0)
    down(3, 0)
    c2_start(3, 0)
    z_copy(1, 1).wait_recv()
    fan_start(1, 1)
    z_copy(3, 1).wait_recv()
    fan_start(3, 1)
    relay_near(2, 0)
    relay_rest(2, 0)
    up(2, 0)
    down(2, 0)
    c2_start(2, 0)
    pick()
    z_copy(2, 1).wait_recv()
    fan_start(2, 1)
    l_copy.start()
    c3_start(1, 0)
    c3_start(3, 0)
    relay_near(1, 1)
    relay_near(3, 1)
    back_start(1, 0)
    back_start(3, 0)
    relay_rest(1, 1)
    relay_rest(3, 1)
    up(1, 1)
    down(1, 1)
    c2_start(1, 1)
    up(3, 1)
    down(3, 1)
    c2_start(3, 1)
    c3_start(2, 0)
    relay_near(2, 1)
    relay_rest(2, 1)
    back_start(2, 0)
    up(2, 1)
    down(2, 1)
    c2_start(2, 1)
    c2_start(0, 0)
    c2_start(0, 1)
    c3_start(1, 1)
    c3_start(3, 1)
    back_start(1, 1)
    back_start(3, 1)
    mix(1, (0,), start=True)
    c3_start(2, 1)
    mix(3, (0,))
    back_start(2, 1)
    mix(2, (0,))
    c3_start(0, 0)
    c3_start(0, 1)
    land()
    mix(1, (1,))
    mix(3, (1,))
    mix(2, (1,))
    mix(0, (0,))
    mix(0, (1,), last=True)
    join(0)
    join(1)
    sib_meta.wait_send()
    for k in range(K):
        sib_tok(k).wait_send()
    for q in range(4):
        for r in range(2):
            away, over, _, beyond = fan(q, r)
            away.wait_send()

            @pl.when(serve == 1)
            def _():
                over.wait_send()

            @pl.when(serve == 0)
            def _():
                beyond.wait_send()

            @pl.when(even(q, r) == 1)
            def _():
                relay(q, r, cross).wait_send()

            @pl.when(even(q, r) == 0)
            def _():
                relay(q, r, near).wait_send()
                relay(q, r, mate).wait_send()

            for cp in c1(q, r):
                cp.wait_send()
            c2(q, r).wait_send()
            away, _, here = c3(q, r)

            @pl.when(here == 0)
            def _():
                away.wait_send()

            if q:
                z_copy(q, r).wait_send()
                back(q, r).wait_send()


def on_device(tokens, expert_ids, gate_weights, donor_group, gate_pieces, up_pieces, down_pieces):
    tok = tokens.reshape(128, D)
    ids = expert_ids.reshape(128, 2).T.astype(F32)
    wts = gate_weights.reshape(128, 2).T
    meta = jnp.concatenate([ids, wts, jnp.zeros((4, 128), F32)], axis=0)
    vmem, hbm = pltpu.VMEM, pl.ANY
    dma = pltpu.SemaphoreType.DMA
    mixed, landed = pl.pallas_call(
        layer,
        out_shape=(
            jax.ShapeDtypeStruct((128, D), BF),
            jax.ShapeDtypeStruct((3, SPAN, F), BF),
        ),
        in_specs=[
            pl.BlockSpec(memory_space=hbm),
            pl.BlockSpec(memory_space=vmem),
            pl.BlockSpec(memory_space=pltpu.SMEM),
            pl.BlockSpec(memory_space=hbm),
            pl.BlockSpec(memory_space=hbm),
            pl.BlockSpec(memory_space=hbm),
        ],
        out_specs=(pl.BlockSpec(memory_space=vmem), pl.BlockSpec(memory_space=vmem)),
        scratch_shapes=[
            vmem((256, D), BF),
            vmem((8, 128), F32),
            vmem((4 * CH, 256), BF),
            vmem((4 * CH, 256), BF),
            vmem((4 * CH, D), BF),
            vmem((3 * CH, D), BF),
            vmem((16 * CH, D), BF),
            vmem((D, F), BF),
            vmem((D, F), BF),
            vmem((D, F), BF),
            vmem((4 * CH, F), F32),
            vmem((4 * CH, F), F32),
            vmem((16 * CH, F), BF),
            vmem((16 * CH, D), BF),
            vmem((8 * CH, D), BF),
            vmem((4 * CH, D), BF),
            vmem((3 * CH, D), BF),
            vmem((4 * CH, D), BF),
            vmem((256, D), F32),
            vmem((128, D), BF),
            vmem((128, D), BF),
            vmem((12, SPAN, F), BF),
            vmem((3, SPAN, F), BF),
            vmem((3, SPAN, F), BF),
            dma((7,)),
            dma, dma,
            dma((K,)), dma((K,)),
            dma((6,)), dma((6,)),
            dma((16,)), dma((32,)), dma((32,)),
            dma((16,)), dma((16,)),
            dma((8,)), dma((8,)),
            dma((8,)), dma((8,)),
            dma((6,)), dma((6,)),
            dma((9,)), dma((9,)),
            dma, dma,
            dma((K,)), dma((K,)),
        ],
        compiler_params=pltpu.CompilerParams(
            collective_id=0, has_side_effects=True, vmem_limit_bytes=62 * 2**20
        ),
        cost_estimate=pl.CostEstimate(
            flops=8 * 10**9, bytes_accessed=10**7, transcendentals=4 * 10**5
        ),
    )(tok, meta, donor_group, gate_pieces[0], up_pieces[0], down_pieces[0])
    return mixed.reshape(2, 64, D), landed


def solution(mesh):
    in_specs = (
        P(None, ("grp", "ep"), None),
        P(None, ("grp", "ep"), None),
        P(None, ("grp", "ep"), None),
        P(),
        P(("grp", "ep"), None, None),
        P(("grp", "ep"), None, None),
        P(("grp", "ep"), None, None),
    )
    out_specs = (P(None, ("grp", "ep"), None), P(None, ("grp", "ep"), None))
    return jax.shard_map(
        on_device, mesh=mesh, in_specs=in_specs, out_specs=out_specs, check_vma=False
    )
```
